32 devices in a mesh: parts: 2 (over y), users: 16 (over z, x, core).
Axes of the slice: x: 2, y: 2, z: 4, core: 2. Of those that a mesh axis runs over, the one named last changes fastest.
Arguments:
- candidates: bfloat16 [512, 512], P(('parts', 'users')), parts along dimension 0, may hold values from -6 to 6
- candidate_user: int32 [512], P(('parts', 'users')), parts along dimension 0, may hold values from 0 to 7
- events: bfloat16 [65536, 512], P(('parts', 'users')), parts along dimension 0, may hold values from -6 to 6
- event_user: int32 [65536], P(('parts', 'users')), parts along dimension 0, may hold values from 0 to 7, never falling along the last dimension, each value on 1 to 12288 neighbouring positions
- event_mask: int32 [65536], P(('parts', 'users')), parts along dimension 0, may hold values 0 or 1
- query_weight: bfloat16 [512, 512], replicated, may hold values from -0.25 to 0.25
- key_weight: bfloat16 [512, 512], replicated, may hold values from -0.25 to 0.25
- value_weight: bfloat16 [512, 512], replicated, may hold values from -2 to 2
- gate_weight: bfloat16 [512, 512], replicated, may hold values from -0.25 to 0.25
- output_weight: bfloat16 [512, 512], replicated, may hold values from -0.25 to 0.25
Outputs:
- candidate_out: bfloat16 [512, 512], P(('parts', 'users')), parts along dimension 0
The draws below stay inside these ranges and needn't reach their ends.
There are 2 independent parts, one for each index of `parts`. The reference program is written for one: setup_inputs(seed, part) draws one part's arguments, and reference() takes and returns one part's arrays. A program takes and returns all parts, laid end to end along the dimension named above; an argument that names none is the same for every part. Nothing has to cross between parts.
Inputs may be any that keep to these rules, and one draw needn't show every extreme that they name: event_user never falls along the events; each user's events form one run of at most 12288 slots.
All inputs are finite; a program needn't handle non-finite values. No bound on the sum of `event_mask` on one device may be relied on, other than what follows from the above.
Results may differ from the reference program's by a relative error of at most 0.0044.
Values may be sent and summed in bfloat16 or wider, within the bound.
A program may use at most 64 MiB of HBM per device.

```python
import math
import jax
import jax.numpy as jnp
import numpy as np
from jax import lax

D = 512
HEADS = 4
DH = 128
USERS = 8
EV_DEV = 2048
CANDS = 256
EVENTS = 32768
MOST = 12288
N_USERS = 16


def draw_value_weight(key, part):
    normal_key, scale_key = jax.random.split(key, 2)
    entries = jnp.clip(jax.random.normal(normal_key, (D, D), jnp.float32), -6.0, 6.0)
    column_scale = jnp.exp(jax.random.uniform(scale_key, (1, D), jnp.float32, jnp.log(0.3), jnp.log(3.0)))
    return (entries * column_scale / jnp.sqrt(D * 1.0)).astype(jnp.bfloat16)


def set_ends(values, own_key, smallest, high):
    place = [jax.random.randint(jax.random.fold_in(own_key, axis), (), 0, length) for axis, length in enumerate(values.shape)]
    longest = values.shape.index(max(values.shape))
    neighbour = place[:longest] + [(place[longest] + 1) % values.shape[longest]] + place[longest + 1:]
    return values.at[tuple(place)].set(smallest).at[tuple(neighbour)].set(high)


def block_levels(key, extent, cuts, smallest, top_value):
    level = 1.0
    for dim, blocks in cuts:
        steps = jax.random.uniform(jax.random.fold_in(jax.random.fold_in(key, 6), dim), (blocks,), jnp.float32, smallest / len(cuts), top_value / len(cuts))
        level = level * jnp.repeat(jnp.exp(steps), extent[dim] // blocks).reshape((-1,) + (1,) * (len(extent) - 1 - dim))
    return level


def length_profile(count, total, limit, skew):
    loads = [(1 << 20) // math.isqrt(standing ** skew) + 1 for standing in range(2, count + 1)]
    surplus, holding = total - limit - (count - 1), [1] * (count - 1)
    while surplus > 0:
        free = [i for i in range(count - 1) if holding[i] < limit]
        whole, remaining = sum([loads[i] for i in free]), surplus
        for i in free:
            more = min(limit - holding[i], max(1, remaining * loads[i] // whole), surplus)
            holding[i] = holding[i] + more
            surplus = surplus - more
    return np.array([limit] + holding)


def uneven_parts(rng, amount, total, limit, skew):
    if amount == 2:
        one = jax.random.randint(rng, (), max(1, total - limit), min(limit, total - 1) + 1)
        return jnp.stack([one, total - one])
    tallies = jnp.asarray(length_profile(amount, total, limit, skew), jnp.int32)
    couples = (amount - 1) // 2
    giver, taker = tallies[1:1 + 2 * couples:2], tallies[2:2 + 2 * couples:2]
    slack = jnp.minimum(giver - 1, limit - taker)
    passed = jax.random.randint(jax.random.fold_in(rng, 1), (couples,), 0, 1 << 20) % (slack + 1)
    tallies = tallies.at[1:1 + 2 * couples:2].set(giver - passed).at[2:2 + 2 * couples:2].set(taker + passed)
    return tallies[jax.random.permutation(jax.random.fold_in(rng, 2), amount)]


def noise(own_key, extent, scale, reach, pieces=(), dtype=jnp.bfloat16):
    level = block_levels(own_key, extent, pieces, -0.22, 0.18) if pieces else 1.0
    array = jax.random.normal(own_key, extent, jnp.float32) * scale * level
    return jnp.minimum(jnp.maximum(array, -reach), reach).astype(dtype)


def setup_inputs(seed: int = 0, part: int = 0) -> dict:
    keys = jax.random.split(jax.random.key(seed), 11)
    own_keys = jax.random.split(jax.random.fold_in(keys[10], part), 11)
    return {
        "candidates": noise(own_keys[0], (CANDS, D), 1.0, 6.0, ((0, 16),)),
        "candidate_user": set_ends(jax.random.randint(own_keys[1], (CANDS,), 0, USERS), jax.random.fold_in(own_keys[1], 1), 0, USERS - 1).astype(jnp.int32),
        "events": noise(own_keys[2], (EVENTS, D), 1.0, 6.0, ((0, 16),)),
        "event_user": jnp.searchsorted(jnp.cumsum(uneven_parts(own_keys[3], USERS, EVENTS, MOST, 2)), jnp.arange(EVENTS), side="right").astype(jnp.int32),
        "event_mask": set_ends((jax.random.randint(own_keys[4], (EVENTS,), 0, 4) < 3).astype(jnp.int32), jax.random.fold_in(own_keys[4], 1), 0, 1),
        "query_weight": noise(keys[5], (D, D), D ** -0.5, 0.25),
        "key_weight": noise(keys[6], (D, D), D ** -0.5, 0.25),
        "value_weight": draw_value_weight(jax.random.fold_in(keys[10], 71), part),
        "gate_weight": noise(keys[8], (D, D), D ** -0.5, 0.25),
        "output_weight": noise(keys[9], (D, D), D ** -0.5, 0.25),
    }


def reference(candidates, candidate_user, events, event_user, event_mask, query_weight, key_weight, value_weight, gate_weight, output_weight):
    queries = jnp.dot(candidates, query_weight, preferred_element_type=jnp.float32).astype(jnp.bfloat16)
    gate_values = jax.nn.silu(jnp.dot(candidates, gate_weight, preferred_element_type=jnp.float32))
    key_rows = jnp.dot(events, key_weight, preferred_element_type=jnp.float32).astype(jnp.bfloat16)
    value_rows = jnp.dot(events, value_weight, preferred_element_type=jnp.float32).astype(jnp.bfloat16)
    score_scale = 1.0 / math.sqrt(DH)
    query_heads = queries.astype(jnp.float32).reshape(CANDS, HEADS, DH)
    key_blocks = key_rows.astype(jnp.float32).reshape(N_USERS, EV_DEV, HEADS, DH)
    value_blocks = value_rows.astype(jnp.float32).reshape(N_USERS, EV_DEV, HEADS, DH)
    user_blocks = event_user.reshape(N_USERS, EV_DEV)
    mask_blocks = event_mask.astype(jnp.float32).reshape(N_USERS, EV_DEV)

    def add_block(summed, block_items):
        key_part, value_part, user_part, mask_part = block_items
        scores = jnp.einsum('chd,ehd->hce', query_heads, key_part) * score_scale
        same_user = (candidate_user[:, None] == user_part[None, :]).astype(jnp.float32) * mask_part[None, :]
        attn_weights = (jax.nn.silu(scores) * same_user[None]).astype(jnp.bfloat16).astype(jnp.float32)
        return (summed + jnp.einsum('hce,ehd->chd', attn_weights, value_part).reshape(CANDS, D), None)
    summed, _ = lax.scan(add_block, jnp.zeros((CANDS, D), jnp.float32), (key_blocks, value_blocks, user_blocks, mask_blocks))
    mean_row = lax.optimization_barrier(jnp.mean(summed, axis=1, keepdims=True))
    centred = summed - mean_row
    var_row = lax.optimization_barrier(jnp.mean(centred * centred, axis=1, keepdims=True))
    normed = centred / jnp.sqrt(var_row + 1e-05)
    gated_rows = (normed * gate_values).astype(jnp.bfloat16)
    result = candidates.astype(jnp.float32) + jnp.dot(gated_rows, output_weight, preferred_element_type=jnp.float32)
    return result.astype(jnp.bfloat16)
```

```python
import functools
import math

import jax
import jax.numpy as jnp
from jax import lax
from jax.experimental import pallas as pl
from jax.experimental.pallas import tpu as pltpu
from jax.sharding import PartitionSpec as P

HEADS = 4
LANES = 128
FAR = -(2.0**60)
LINK = jnp.float32
F32 = jnp.float32
BF16 = jnp.bfloat16


def divisor(total, wanted):
    return math.gcd(total, wanted)


def kernel(
    n,
    cand_hbm,
    cuser_hbm,
    ev_hbm,
    euser_hbm,
    emask_hbm,
    wq_hbm,
    wk_hbm,
    wv_hbm,
    wg_hbm,
    wo_hbm,
    out_ref,
    cand,
    cuser,
    ev,
    euser,
    emask,
    wq,
    wk,
    wv,
    wg,
    wo,
    q_all,
    keys,
    vals,
    gate,
    part,
    sib,
    chip,
    land,
    in_sem,
    ev_sem,
    q_send,
    q_recv,
    f_sem,
    s_send,
    s_recv,
    r_send,
    r_recv,
):
    chips = n // 2
    rows, width = cand.shape
    dh = width // HEADS
    events = ev.shape[0]
    chunk = divisor(events, 512)
    ev_chunks = events // chunk
    half_scale = 0.5 / math.sqrt(dh)

    me = lax.axis_index("users")
    k = me // 2
    c = lax.rem(me, 2)
    other = 1 - c
    sibling = {"users": k * 2 + other}

    def peer_of(i):
        return lax.rem(k + i, chips)

    small = [
        (cand_hbm, cand),
        (cuser_hbm, cuser),
        (wq_hbm, wq),
        (euser_hbm, euser),
        (emask_hbm, emask),
        (wk_hbm, wk),
        (wv_hbm, wv),
        (wg_hbm, wg),
        (wo_hbm, wo),
    ]
    copies = [pltpu.make_async_copy(s, d, in_sem.at[i]) for i, (s, d) in enumerate(small)]
    ev_copies = [
        pltpu.make_async_copy(
            ev_hbm.at[pl.ds(j * chunk, chunk)], ev.at[pl.ds(j * chunk, chunk)], ev_sem.at[j]
        )
        for j in range(ev_chunks)
    ]

    barrier = pltpu.get_barrier_semaphore()

    @pl.loop(1, chips)
    def _(i):
        pl.semaphore_signal(barrier, inc=1, device_id={"users": peer_of(i) * 2 + c})

    pl.semaphore_signal(barrier, inc=1, device_id=sibling)

    for copy in copies[:6]:
        copy.start()
    for copy in ev_copies:
        copy.start()
    for copy in copies[6:]:
        copy.start()

    for copy in copies[:3]:
        copy.wait()
    queries = jnp.dot(cand[...], wq[...], preferred_element_type=F32).astype(BF16)
    diagonal = lax.broadcasted_iota(jnp.int32, (rows, rows), 0) == lax.broadcasted_iota(
        jnp.int32, (rows, rows), 1
    )
    user_col = jnp.sum(
        jnp.where(diagonal, jnp.broadcast_to(cuser[...].astype(F32), (rows, rows)), 0.0),
        axis=1,
        keepdims=True,
    )
    lane_ids = lax.broadcasted_iota(jnp.int32, (rows, LANES), 1).astype(F32)
    one_hot = jnp.where(lane_ids == user_col, 1.0, 0.0).astype(BF16)
    mine = c * chips + k
    q_all[mine, :, pl.ds(0, width)] = queries
    q_all[mine, :, pl.ds(width, LANES)] = one_hot

    pl.semaphore_wait(barrier, chips)

    def q_copy(i):
        peer = peer_of(i)
        return pltpu.make_async_remote_copy(
            src_ref=q_all.at[mine],
            dst_ref=q_all.at[mine],
            send_sem=q_send.at[peer],
            recv_sem=q_recv.at[k],
            device_id={"users": peer * 2 + c},
        )

    def q_arrival(i):
        peer = peer_of(i)
        slot = q_all.at[c * chips + peer]
        return pltpu.make_async_remote_copy(
            src_ref=slot,
            dst_ref=slot,
            send_sem=q_send.at[peer],
            recv_sem=q_recv.at[peer],
            device_id={"users": peer * 2 + c},
        )

    @pl.loop(1, chips)
    def _(i):
        q_copy(i).start()

    copies[3].wait()
    copies[4].wait()
    for j in range(ev_chunks):
        at = pl.ds(j * chunk, chunk)
        eff = jnp.where(emask[:, at] == 1, euser[:, at], -1)
        ids = lax.broadcasted_iota(jnp.int32, (LANES, chunk), 0)
        miss = jnp.where(ids == eff, 0.0, FAR)
        miss = miss.T.astype(BF16)
        for h in range(HEADS):
            keys[h, at, pl.ds(dh, LANES)] = miss

    copies[5].wait()
    for j in range(ev_chunks):
        at = pl.ds(j * chunk, chunk)
        ev_copies[j].wait()
        rows_k = jnp.dot(ev[at, :], wk[...], preferred_element_type=F32).astype(BF16)
        for h in range(HEADS):
            keys[h, at, pl.ds(0, dh)] = rows_k[:, h * dh : (h + 1) * dh]

    @pl.loop(1, chips)
    def _(i):
        q_arrival(i).wait_recv()

    def forward(core):
        block = q_all.at[pl.ds(core * chips, chips)]
        return pltpu.make_async_remote_copy(
            src_ref=block,
            dst_ref=block,
            send_sem=f_sem.at[0],
            recv_sem=f_sem.at[1],
            device_id=sibling,
        )

    forward(c).start()

    copies[6].wait()
    for j in range(ev_chunks):
        at = pl.ds(j * chunk, chunk)
        vals[at, :] = jnp.dot(ev[at, :], wv[...], preferred_element_type=F32).astype(BF16)

    copies[7].wait()
    pre = 0.5 * jnp.dot(cand[...], wg[...], preferred_element_type=F32)
    gate[...] = pre + pre * jnp.tanh(pre)
    copies[8].wait()

    forward(other).wait_recv()

    total = n * rows
    block = divisor(total, 256)
    slots = block // rows

    def attention(h, b):
        at_slots = pl.ds(b * slots, slots)
        q = q_all[at_slots].reshape(block, width + LANES)
        q = jnp.concatenate([q[:, h * dh : (h + 1) * dh], q[:, width:]], axis=1)
        acc = None
        for j in range(ev_chunks):
            at = pl.ds(j * chunk, chunk)
            raw = lax.dot_general(
                q, keys[h, at, :], (((1,), (1,)), ((), ())), preferred_element_type=F32
            )
            s = raw * half_scale
            attn = (s + s * jnp.tanh(s)).astype(BF16)
            term = jnp.dot(attn, vals[at, pl.ds(h * dh, dh)], preferred_element_type=F32)
            acc = term if acc is None else acc + term
        part[h, at_slots] = acc.reshape(slots, rows, dh)

    def to_sibling(h, core):
        return pltpu.make_async_remote_copy(
            src_ref=part.at[h, pl.ds(core * chips, chips)],
            dst_ref=sib.at[h],
            send_sem=s_send.at[h],
            recv_sem=s_recv.at[h],
            device_id=sibling,
        )

    def to_chip(h, i):
        peer = peer_of(i)
        return pltpu.make_async_remote_copy(
            src_ref=chip.at[h, peer],
            dst_ref=land.at[h, k],
            send_sem=r_send.at[h, peer],
            recv_sem=r_recv.at[h, k],
            device_id={"users": peer * 2 + c},
        )

    def from_chip(h, i):
        peer = peer_of(i)
        return pltpu.make_async_remote_copy(
            src_ref=chip.at[h, peer],
            dst_ref=land.at[h, peer],
            send_sem=r_send.at[h, peer],
            recv_sem=r_recv.at[h, peer],
            device_id={"users": peer * 2 + c},
        )

    def pass_on(h):
        to_sibling(h, other).wait_recv()
        both = part[h, pl.ds(c * chips, chips)] + sib[h]
        chip[h] = both.astype(LINK)

        @pl.loop(1, chips)
        def _(i):
            to_chip(h, i).start()

        land[h, k] = chip[h, k]

    for h in range(HEADS):
        if total == block:
            attention(h, 0)
        else:
            pl.loop(0, total // block)(functools.partial(attention, h))
        to_sibling(h, other).start()
        if h:
            pass_on(h - 1)
    pass_on(HEADS - 1)

    sums = []
    for h in range(HEADS):

        @pl.loop(1, chips)
        def _(i):
            from_chip(h, i).wait_recv()

        sums.append(jnp.sum(land[h].astype(F32), axis=0))
    summed = jnp.concatenate(sums, axis=1)
    mean = jnp.mean(summed, axis=1, keepdims=True)
    centred = summed - mean
    var = jnp.mean(centred * centred, axis=1, keepdims=True)
    normed = centred / jnp.sqrt(var + 1e-5)
    gated = (normed * gate[...]).astype(BF16)
    result = cand[...].astype(F32) + jnp.dot(gated, wo[...], preferred_element_type=F32)
    out_ref[...] = result.astype(out_ref.dtype)

    @pl.loop(1, chips)
    def _(i):
        q_copy(i).wait_send()

    forward(c).wait_send()
    for h in range(HEADS):
        to_sibling(h, other).wait_send()

        @pl.loop(1, chips)
        def _(i):
            to_chip(h, i).wait_send()


def per_device(
    n,
    candidates,
    candidate_user,
    events,
    event_user,
    event_mask,
    query_weight,
    key_weight,
    value_weight,
    gate_weight,
    output_weight,
):
    rows, width = candidates.shape
    count = events.shape[0]
    chips = n // 2
    dh = width // HEADS
    chunks = count // divisor(count, 512)
    square = pltpu.VMEM((width, width), BF16)
    dma = pltpu.SemaphoreType.DMA
    return pl.pallas_call(
        functools.partial(kernel, n),
        out_shape=jax.ShapeDtypeStruct((rows, width), BF16),
        in_specs=[pl.BlockSpec(memory_space=pl.ANY)] * 10,
        out_specs=pl.BlockSpec(memory_space=pltpu.VMEM),
        scratch_shapes=[
            pltpu.VMEM((rows, width), BF16),
            pltpu.VMEM((1, rows), jnp.int32),
            pltpu.VMEM((count, width), BF16),
            pltpu.VMEM((1, count), jnp.int32),
            pltpu.VMEM((1, count), jnp.int32),
            square,
            square,
            square,
            square,
            square,
            pltpu.VMEM((n, rows, width + LANES), BF16),
            pltpu.VMEM((HEADS, count, dh + LANES), BF16),
            pltpu.VMEM((count, width), BF16),
            pltpu.VMEM((rows, width), F32),
            pltpu.VMEM((HEADS, n, rows, dh), F32),
            pltpu.VMEM((HEADS, chips, rows, dh), F32),
            pltpu.VMEM((HEADS, chips, rows, dh), LINK),
            pltpu.VMEM((HEADS, chips, rows, dh), LINK),
            dma((9,)),
            dma((chunks,)),
            dma((chips,)),
            dma((chips,)),
            dma((2,)),
            dma((HEADS,)),
            dma((HEADS,)),
            dma((HEADS, chips)),
            dma((HEADS, chips)),
        ],
        compiler_params=pltpu.CompilerParams(
            collective_id=0, has_side_effects=True, vmem_limit_bytes=56 * 2**20
        ),
    )(
        candidates,
        candidate_user.reshape(1, rows),
        events,
        event_user.reshape(1, count),
        event_mask.reshape(1, count),
        query_weight,
        key_weight,
        value_weight,
        gate_weight,
        output_weight,
    )


def solution(mesh):
    spread = ("parts", "users")
    in_specs = (P(spread, None), P(spread), P(spread, None), P(spread), P(spread)) + (P(),) * 5
    return jax.shard_map(
        functools.partial(per_device, mesh.shape["users"]),
        mesh=mesh,
        in_specs=in_specs,
        out_specs=P(spread, None),
        check_vma=False,
    )
```

```python
import functools
import math

import jax
import jax.numpy as jnp
from jax import lax
from jax.experimental import pallas as pl
from jax.experimental.pallas import tpu as pltpu
from jax.sharding import PartitionSpec as P

HEADS = 4
LANES = 128
FAR = -(2.0**60)
LINK = jnp.bfloat16
F32 = jnp.float32
BF16 = jnp.bfloat16


def divisor(total, wanted):
    return math.gcd(total, wanted)


def kernel(
    n,
    cand_hbm,
    cuser_hbm,
    ev_hbm,
    euser_hbm,
    emask_hbm,
    wq_hbm,
    wk_hbm,
    wv_hbm,
    wg_hbm,
    wo_hbm,
    out_ref,
    cand,
    cuser,
    ev,
    euser,
    emask,
    wq,
    wkv,
    wg,
    wo,
    q_own,
    q_all,
    users,
    keys,
    vals,
    gate,
    part,
    land,
    in_sem,
    ev_sem,
    q_send,
    q_recv,
    u_send,
    u_recv,
    e_send,
    e_recv,
    r_send,
    r_recv,
):
    rows, width = cand.shape
    half = width // 2
    dh = width // HEADS
    pair = HEADS // 2
    events = ev.shape[1]
    chunk = divisor(events, 512)
    ev_chunks = events // chunk
    half_scale = 0.5 / math.sqrt(dh)

    me = lax.axis_index("users")
    c = lax.rem(me, 2)
    other = 1 - c
    sib_id = me - c + other
    sibling = {"users": sib_id}
    columns = pl.ds(pl.multiple_of(c * half, half), half)

    def peer_of(i):
        return lax.rem(me + i, n)

    small = [
        (cand_hbm, cand),
        (cuser_hbm, cuser),
        (wq_hbm, wq),
        (euser_hbm, euser.at[0]),
        (emask_hbm, emask.at[0]),
        (wk_hbm.at[:, columns], wkv.at[:, pl.ds(0, half)]),
        (wv_hbm.at[:, columns], wkv.at[:, pl.ds(half, half)]),
        (wg_hbm, wg),
        (wo_hbm, wo),
    ]
    copies = [pltpu.make_async_copy(s, d, in_sem.at[i]) for i, (s, d) in enumerate(small)]
    ev_copies = [
        pltpu.make_async_copy(
            ev_hbm.at[pl.ds(j * chunk, chunk)], ev.at[0, pl.ds(j * chunk, chunk)], ev_sem.at[j]
        )
        for j in range(ev_chunks)
    ]

    barrier = pltpu.get_barrier_semaphore()

    @pl.loop(1, n)
    def _(i):
        pl.semaphore_signal(barrier, inc=1, device_id={"users": peer_of(i)})

    for copy in copies[:5]:
        copy.start()
    for copy in ev_copies:
        copy.start()
    for copy in copies[5:]:
        copy.start()

    for copy in copies[:3]:
        copy.wait()
    queries = jnp.dot(cand[...], wq[...], preferred_element_type=F32).astype(BF16)
    for core in range(2):
        q_own[core] = queries[:, core * half : (core + 1) * half]
    q_all[me] = q_own[c]
    users[me] = jnp.zeros((1, LANES), jnp.int32)
    users[me, :, pl.ds(0, rows)] = cuser[...]
    copies[3].wait()
    copies[4].wait()
    for copy in ev_copies:
        copy.wait()

    pl.semaphore_wait(barrier, n - 1)

    def q_copy(i):
        peer = peer_of(i)
        return pltpu.make_async_remote_copy(
            src_ref=q_own.at[lax.rem(peer, 2)],
            dst_ref=q_all.at[me],
            send_sem=q_send.at[peer],
            recv_sem=q_recv.at[me],
            device_id={"users": peer},
        )

    def u_copy(i):
        peer = peer_of(i)
        return pltpu.make_async_remote_copy(
            src_ref=users.at[me],
            dst_ref=users.at[me],
            send_sem=u_send.at[peer],
            recv_sem=u_recv.at[me],
            device_id={"users": peer},
        )

    def q_arrival(i):
        peer = peer_of(i)
        return pltpu.make_async_remote_copy(
            src_ref=q_own.at[0],
            dst_ref=q_all.at[peer],
            send_sem=q_send.at[peer],
            recv_sem=q_recv.at[peer],
            device_id={"users": peer},
        )

    def u_arrival(i):
        peer = peer_of(i)
        return pltpu.make_async_remote_copy(
            src_ref=users.at[me],
            dst_ref=users.at[peer],
            send_sem=u_send.at[peer],
            recv_sem=u_recv.at[peer],
            device_id={"users": peer},
        )

    def event_copy(j):
        at = pl.ds(j * chunk, chunk)
        return pltpu.make_async_remote_copy(
            src_ref=ev.at[0, at],
            dst_ref=ev.at[1, at],
            send_sem=e_send.at[j],
            recv_sem=e_recv.at[j],
            device_id=sibling,
        )

    def tag_copy(ref, j):
        return pltpu.make_async_remote_copy(
            src_ref=ref.at[0],
            dst_ref=ref.at[1],
            send_sem=e_send.at[j],
            recv_sem=e_recv.at[j],
            device_id=sibling,
        )

    handed = [event_copy(j) for j in range(ev_chunks)]
    tags = [tag_copy(euser, ev_chunks), tag_copy(emask, ev_chunks + 1)]
    handed[0].start()

    @pl.loop(1, n)
    def _(i):
        q_copy(i).start()
        u_copy(i).start()

    for copy in tags:
        copy.start()
    for copy in handed[1:]:
        copy.start()

    def keys_and_values(e):
        for j in range(ev_chunks):
            at = pl.ds(j * chunk, chunk)
            if e:
                handed[j].wait_recv()
            both = jnp.dot(ev[e, at, :], wkv[...], preferred_element_type=F32).astype(BF16)
            for h in range(pair):
                keys[h, e, at, pl.ds(0, dh)] = both[:, h * dh : (h + 1) * dh]
            vals[e, at, :] = both[:, half:]

    def mask_columns(e):
        for j in range(ev_chunks):
            at = pl.ds(j * chunk, chunk)
            eff = jnp.where(emask[e, :, at] == 1, euser[e, :, at], -1)
            ids = lax.broadcasted_iota(jnp.int32, (LANES, chunk), 0)
            miss = jnp.where(ids == eff, 0.0, FAR).T.astype(BF16)
            for h in range(pair):
                keys[h, e, at, pl.ds(dh, LANES)] = miss

    copies[5].wait()
    copies[6].wait()
    mask_columns(0)
    keys_and_values(0)

    copies[7].wait()
    pre = 0.5 * jnp.dot(cand[...], wg[...], preferred_element_type=F32)
    gate[...] = pre + pre * jnp.tanh(pre)
    copies[8].wait()

    for copy in tags:
        copy.wait_recv()
    mask_columns(1)
    keys_and_values(1)

    @pl.loop(1, n)
    def _(i):
        q_arrival(i).wait_recv()
        u_arrival(i).wait_recv()

    total = n * rows
    block = divisor(total, 256)
    slots = block // rows

    def attention(g, b):
        at_slots = pl.ds(b * slots, slots)
        q = q_all[at_slots].reshape(block, half)[:, g * dh : (g + 1) * dh]
        shape = (slots, rows, LANES)
        own_lane = lax.broadcasted_iota(jnp.int32, shape, 1) == lax.broadcasted_iota(
            jnp.int32, shape, 2
        )
        spread = jnp.where(own_lane, jnp.broadcast_to(users[at_slots], shape).astype(F32), 0.0)
        user_col = jnp.sum(spread, axis=2, keepdims=True)
        lane_ids = lax.broadcasted_iota(jnp.int32, shape, 2).astype(F32)
        one_hot = jnp.where(lane_ids == user_col, 1.0, 0.0).reshape(block, LANES).astype(BF16)
        q = jnp.concatenate([q, one_hot], axis=1)
        acc = None
        for e in range(2):
            for j in range(ev_chunks):
                at = pl.ds(j * chunk, chunk)
                raw = lax.dot_general(
                    q, keys[g, e, at, :], (((1,), (1,)), ((), ())), preferred_element_type=F32
                )
                s = raw * half_scale
                attn = (s + s * jnp.tanh(s)).astype(BF16)
                term = jnp.dot(
                    attn, vals[e, at, pl.ds(g * dh, dh)], preferred_element_type=F32
                )
                acc = term if acc is None else acc + term
        part[g, at_slots] = acc.reshape(slots, rows, dh).astype(LINK)

    def give(g, i):
        peer = peer_of(i)
        return pltpu.make_async_remote_copy(
            src_ref=part.at[g, peer],
            dst_ref=land.at[g, me],
            send_sem=r_send.at[g, peer],
            recv_sem=r_recv.at[g, me],
            device_id={"users": peer},
        )

    def take(g, i):
        peer = peer_of(i)
        return pltpu.make_async_remote_copy(
            src_ref=part.at[g, peer],
            dst_ref=land.at[g, peer],
            send_sem=r_send.at[g, peer],
            recv_sem=r_recv.at[g, peer],
            device_id={"users": peer},
        )

    for g in range(pair):
        if total == block:
            attention(g, 0)
        else:
            pl.loop(0, total // block)(functools.partial(attention, g))

        @pl.loop(1, n)
        def _(i):
            give(g, i).start()

        land[g, me] = part[g, me]

    @pl.loop(1, n)
    def _(i):
        q_copy(i).wait_send()
        u_copy(i).wait_send()

    for copy in handed + tags:
        copy.wait_send()

    sums = []
    for g in range(pair):

        @pl.loop(1, n)
        def _(i):
            take(g, i).wait_recv()

        landed = land[g].astype(F32).reshape(n // 2, 2, rows, dh)
        sums.append(jnp.sum(landed, axis=0))
    summed = jnp.concatenate([sums[g][core] for core in range(2) for g in range(pair)], axis=1)
    mean = jnp.mean(summed, axis=1, keepdims=True)
    centred = summed - mean
    var = jnp.mean(centred * centred, axis=1, keepdims=True)
    normed = centred / jnp.sqrt(var + 1e-5)
    gated = (normed * gate[...]).astype(BF16)
    out_ref[...] = jnp.dot(gated, wo[...], preferred_element_type=F32)

    for g in range(pair):

        @pl.loop(1, n)
        def _(i):
            give(g, i).wait_send()


def per_device(
    n,
    candidates,
    candidate_user,
    events,
    event_user,
    event_mask,
    query_weight,
    key_weight,
    value_weight,
    gate_weight,
    output_weight,
):
    rows, width = candidates.shape
    count = events.shape[0]
    half = width // 2
    pair = HEADS // 2
    dh = width // HEADS
    chunks = count // divisor(count, 512)
    square = pltpu.VMEM((width, width), BF16)
    dma = pltpu.SemaphoreType.DMA
    delta = pl.pallas_call(
        functools.partial(kernel, n),
        out_shape=jax.ShapeDtypeStruct((rows, width), F32),
        in_specs=[pl.BlockSpec(memory_space=pl.ANY)] * 10,
        out_specs=pl.BlockSpec(memory_space=pltpu.VMEM),
        scratch_shapes=[
            pltpu.VMEM((rows, width), BF16),
            pltpu.VMEM((1, rows), jnp.int32),
            pltpu.VMEM((2, count, width), BF16),
            pltpu.VMEM((2, 1, count), jnp.int32),
            pltpu.VMEM((2, 1, count), jnp.int32),
            square,
            square,
            square,
            square,
            pltpu.VMEM((2, rows, half), BF16),
            pltpu.VMEM((n, rows, half), BF16),
            pltpu.VMEM((n, 1, LANES), jnp.int32),
            pltpu.VMEM((pair, 2, count, dh + LANES), BF16),
            pltpu.VMEM((2, count, half), BF16),
            pltpu.VMEM((rows, width), F32),
            pltpu.VMEM((pair, n, rows, dh), LINK),
            pltpu.VMEM((pair, n, rows, dh), LINK),
            dma((9,)),
            dma((chunks,)),
            dma((n,)),
            dma((n,)),
            dma((n,)),
            dma((n,)),
            dma((chunks + 2,)),
            dma((chunks + 2,)),
            dma((pair, n)),
            dma((pair, n)),
        ],
        compiler_params=pltpu.CompilerParams(
            collective_id=0, has_side_effects=True, vmem_limit_bytes=56 * 2**20
        ),
    )(
        candidates,
        candidate_user.reshape(1, rows),
        events,
        event_user.reshape(1, count),
        event_mask.reshape(1, count),
        query_weight,
        key_weight,
        value_weight,
        gate_weight,
        output_weight,
    )
    return (candidates.astype(F32) + delta).astype(BF16)


def solution(mesh):
    spread = ("parts", "users")
    in_specs = (P(spread, None), P(spread), P(spread, None), P(spread), P(spread)) + (P(),) * 5
    return jax.shard_map(
        functools.partial(per_device, mesh.shape["users"]),
        mesh=mesh,
        in_specs=in_specs,
        out_specs=P(spread, None),
        check_vma=False,
    )
```

```python
import functools
import math

import jax
import jax.numpy as jnp
from jax import lax
from jax.experimental import pallas as pl
from jax.experimental.pallas import tpu as pltpu
from jax.sharding import PartitionSpec as P

HEADS = 4
LANES = 128
FAR = -(2.0**60)
LINK = jnp.bfloat16
F32 = jnp.float32
BF16 = jnp.bfloat16


def divisor(total, wanted):
    return math.gcd(total, wanted)


def each_peer(n, body):
    if n <= 32:
        for i in sorted(range(1, n), key=lambda i: abs(i - n // 2)):
            body(i)
    else:
        pl.loop(1, n)(body)


def kernel(
    n,
    cand_hbm,
    cuser_hbm,
    ev_hbm,
    euser_hbm,
    emask_hbm,
    wq_hbm,
    wk_hbm,
    wv_hbm,
    wg_hbm,
    wo_hbm,
    out_ref,
    cand,
    cuser,
    ev,
    euser,
    emask,
    wq,
    wkv,
    wg,
    wo,
    q_own,
    q_all,
    users,
    hot,
    keys,
    vals,
    gate,
    part,
    land,
    in_sem,
    ev_sem,
    q_send,
    q_recv,
    u_send,
    u_recv,
    e_send,
    e_recv,
    r_send,
    r_recv,
):
    rows, width = cand.shape
    half = width // 2
    dh = width // HEADS
    pair = HEADS // 2
    events = ev.shape[1]
    chunk = divisor(events, 512)
    ev_chunks = events // chunk
    half_scale = 0.5 / math.sqrt(dh)

    me = lax.axis_index("users")
    c = lax.rem(me, 2)
    other = 1 - c
    sib_id = me - c + other
    sibling = {"users": sib_id}
    columns = pl.ds(pl.multiple_of(c * half, half), half)

    def peer_of(i):
        return lax.rem(me + i, n)

    small = [
        (cand_hbm, cand),
        (cuser_hbm, cuser),
        (wq_hbm, wq),
        (euser_hbm, euser.at[0]),
        (emask_hbm, emask.at[0]),
        (wk_hbm.at[:, columns], wkv.at[:, pl.ds(0, half)]),
        (wv_hbm.at[:, columns], wkv.at[:, pl.ds(half, half)]),
        (wg_hbm, wg),
        (wo_hbm, wo),
    ]
    copies = [pltpu.make_async_copy(s, d, in_sem.at[i]) for i, (s, d) in enumerate(small)]
    ev_copies = [
        pltpu.make_async_copy(
            ev_hbm.at[pl.ds(j * chunk, chunk)], ev.at[0, pl.ds(j * chunk, chunk)], ev_sem.at[j]
        )
        for j in range(ev_chunks)
    ]

    barrier = pltpu.get_barrier_semaphore()

    each_peer(
        n, lambda i: pl.semaphore_signal(barrier, inc=1, device_id={"users": peer_of(i)})
    )

    for copy in copies[:5]:
        copy.start()
    for copy in ev_copies:
        copy.start()
    for copy in copies[5:]:
        copy.start()

    for copy in copies[:3]:
        copy.wait()
    queries = jnp.dot(cand[...], wq[...], preferred_element_type=F32).astype(BF16)
    for core in range(2):
        q_own[core] = queries[:, core * half : (core + 1) * half]
    q_all[me] = q_own[c]
    users[me] = jnp.zeros((1, LANES), jnp.int32)
    users[me, :, pl.ds(0, rows)] = cuser[...]

    pl.semaphore_wait(barrier, n - 1)

    def q_copy(i):
        peer = peer_of(i)
        return pltpu.make_async_remote_copy(
            src_ref=q_own.at[lax.rem(peer, 2)],
            dst_ref=q_all.at[me],
            send_sem=q_send.at[0],
            recv_sem=q_recv.at[0],
            device_id={"users": peer},
        )

    def u_copy(i):
        peer = peer_of(i)
        return pltpu.make_async_remote_copy(
            src_ref=users.at[me],
            dst_ref=users.at[me],
            send_sem=u_send.at[0],
            recv_sem=u_recv.at[0],
            device_id={"users": peer},
        )

    def all_of(ref, send_sem, recv_sem):
        block = ref.at[pl.ds(0, n - 1)]
        return pltpu.make_async_remote_copy(
            src_ref=block,
            dst_ref=block,
            send_sem=send_sem,
            recv_sem=recv_sem,
            device_id=sibling,
        )

    all_q = all_of(q_all, q_send.at[0], q_recv.at[0])
    all_u = all_of(users, u_send.at[0], u_recv.at[0])

    def event_copy(j):
        at = pl.ds(j * chunk, chunk)
        return pltpu.make_async_remote_copy(
            src_ref=ev.at[0, at],
            dst_ref=ev.at[1, at],
            send_sem=e_send.at[j],
            recv_sem=e_recv.at[j],
            device_id=sibling,
        )

    def tag_copy(ref, j):
        return pltpu.make_async_remote_copy(
            src_ref=ref.at[0],
            dst_ref=ref.at[1],
            send_sem=e_send.at[j],
            recv_sem=e_recv.at[j],
            device_id=sibling,
        )

    handed = [event_copy(j) for j in range(ev_chunks)]
    tags = [tag_copy(euser, ev_chunks), tag_copy(emask, ev_chunks + 1)]
    each_peer(n, lambda i: q_copy(i).start())
    for local, copy in zip(ev_copies, handed):
        local.wait()
        copy.start()
    copies[3].wait()
    copies[4].wait()
    for copy in tags:
        copy.start()
    each_peer(n, lambda i: u_copy(i).start())

    def keys_and_values(e):
        for j in range(ev_chunks):
            at = pl.ds(j * chunk, chunk)
            if e:
                handed[j].wait_recv()
            both = jnp.dot(ev[e, at, :], wkv[...], preferred_element_type=F32).astype(BF16)
            for h in range(pair):
                keys[h, e, at, pl.ds(0, dh)] = both[:, h * dh : (h + 1) * dh]
            vals[e, at, :] = both[:, half:]

    def mask_columns(e):
        for j in range(ev_chunks):
            at = pl.ds(j * chunk, chunk)
            eff = jnp.where(emask[e, :, at] == 1, euser[e, :, at], -1)
            ids = lax.broadcasted_iota(jnp.int32, (LANES, chunk), 0)
            miss = jnp.where(ids == eff, 0.0, FAR).T.astype(BF16)
            for h in range(pair):
                keys[h, e, at, pl.ds(dh, LANES)] = miss

    copies[5].wait()
    copies[6].wait()
    mask_columns(0)
    keys_and_values(0)

    copies[7].wait()
    pre = 0.5 * jnp.dot(cand[...], wg[...], preferred_element_type=F32)
    gate[...] = pre + pre * jnp.tanh(pre)
    copies[8].wait()

    for copy in tags:
        copy.wait_recv()
    mask_columns(1)
    keys_and_values(1)

    total = n * rows
    block = divisor(total, 256)
    slots = block // rows

    all_u.wait_recv()

    def one_hot(b):
        at_slots = pl.ds(b * slots, slots)
        shape = (slots, rows, LANES)
        own_lane = lax.broadcasted_iota(jnp.int32, shape, 1) == lax.broadcasted_iota(
            jnp.int32, shape, 2
        )
        spread = jnp.where(own_lane, jnp.broadcast_to(users[at_slots], shape).astype(F32), 0.0)
        user_col = jnp.sum(spread, axis=2, keepdims=True)
        lane_ids = lax.broadcasted_iota(jnp.int32, shape, 2).astype(F32)
        hot[at_slots] = jnp.where(lane_ids == user_col, 1.0, 0.0).astype(BF16)

    if total == block:
        one_hot(0)
    else:
        pl.loop(0, total // block)(one_hot)

    all_q.wait_recv()

    def attention(g, b):
        at_slots = pl.ds(b * slots, slots)
        q = q_all[at_slots].reshape(block, half)[:, g * dh : (g + 1) * dh]
        q = jnp.concatenate([q, hot[at_slots].reshape(block, LANES)], axis=1)
        acc = None
        for e in range(2):
            for j in range(ev_chunks):
                at = pl.ds(j * chunk, chunk)
                raw = lax.dot_general(
                    q, keys[g, e, at, :], (((1,), (1,)), ((), ())), preferred_element_type=F32
                )
                s = raw * half_scale
                attn = (s + s * jnp.tanh(s)).astype(BF16)
                term = jnp.dot(
                    attn, vals[e, at, pl.ds(g * dh, dh)], preferred_element_type=F32
                )
                acc = term if acc is None else acc + term
        part[g, at_slots] = acc.reshape(slots, rows, dh).astype(LINK)

    def give(g, i):
        peer = peer_of(i)
        return pltpu.make_async_remote_copy(
            src_ref=part.at[g, peer],
            dst_ref=land.at[g, me],
            send_sem=r_send.at[g],
            recv_sem=r_recv.at[g],
            device_id={"users": peer},
        )

    given = [all_of(land.at[g], r_send.at[g], r_recv.at[g]) for g in range(pair)]

    for g in range(pair):
        if total == block:
            attention(g, 0)
        else:
            pl.loop(0, total // block)(functools.partial(attention, g))

        each_peer(n, functools.partial(lambda g, i: give(g, i).start(), g))
        land[g, me] = part[g, me]

    all_q.wait_send()
    all_u.wait_send()
    for copy in handed + tags:
        copy.wait_send()

    sums = []
    for g in range(pair):
        given[g].wait_recv()
        landed = land[g].astype(F32).reshape(n // 2, 2, rows, dh)
        sums.append(jnp.sum(landed, axis=0))
    summed = jnp.concatenate([sums[g][core] for core in range(2) for g in range(pair)], axis=1)
    mean = jnp.mean(summed, axis=1, keepdims=True)
    centred = summed - mean
    var = jnp.mean(centred * centred, axis=1, keepdims=True)
    normed = centred / jnp.sqrt(var + 1e-5)
    gated = (normed * gate[...]).astype(BF16)
    out_ref[...] = jnp.dot(gated, wo[...], preferred_element_type=F32)

    for copy in given:
        copy.wait_send()


def per_device(
    n,
    candidates,
    candidate_user,
    events,
    event_user,
    event_mask,
    query_weight,
    key_weight,
    value_weight,
    gate_weight,
    output_weight,
):
    rows, width = candidates.shape
    count = events.shape[0]
    half = width // 2
    pair = HEADS // 2
    dh = width // HEADS
    chunks = count // divisor(count, 512)
    square = pltpu.VMEM((width, width), BF16)
    dma = pltpu.SemaphoreType.DMA
    delta = pl.pallas_call(
        functools.partial(kernel, n),
        out_shape=jax.ShapeDtypeStruct((rows, width), F32),
        in_specs=[pl.BlockSpec(memory_space=pl.ANY)] * 10,
        out_specs=pl.BlockSpec(memory_space=pltpu.VMEM),
        scratch_shapes=[
            pltpu.VMEM((rows, width), BF16),
            pltpu.VMEM((1, rows), jnp.int32),
            pltpu.VMEM((2, count, width), BF16),
            pltpu.VMEM((2, 1, count), jnp.int32),
            pltpu.VMEM((2, 1, count), jnp.int32),
            square,
            square,
            square,
            square,
            pltpu.VMEM((2, rows, half), BF16),
            pltpu.VMEM((n, rows, half), BF16),
            pltpu.VMEM((n, 1, LANES), jnp.int32),
            pltpu.VMEM((n, rows, LANES), BF16),
            pltpu.VMEM((pair, 2, count, dh + LANES), BF16),
            pltpu.VMEM((2, count, half), BF16),
            pltpu.VMEM((rows, width), F32),
            pltpu.VMEM((pair, n, rows, dh), LINK),
            pltpu.VMEM((pair, n, rows, dh), LINK),
            dma((9,)),
            dma((chunks,)),
            dma((1,)),
            dma((1,)),
            dma((1,)),
            dma((1,)),
            dma((chunks + 2,)),
            dma((chunks + 2,)),
            dma((pair,)),
            dma((pair,)),
        ],
        compiler_params=pltpu.CompilerParams(
            collective_id=0, has_side_effects=True, vmem_limit_bytes=56 * 2**20
        ),
    )(
        candidates,
        candidate_user.reshape(1, rows),
        events,
        event_user.reshape(1, count),
        event_mask.reshape(1, count),
        query_weight,
        key_weight,
        value_weight,
        gate_weight,
        output_weight,
    )
    return (candidates.astype(F32) + delta).astype(BF16)


def solution(mesh):
    spread = ("parts", "users")
    in_specs = (P(spread, None), P(spread), P(spread, None), P(spread), P(spread)) + (P(),) * 5
    return jax.shard_map(
        functools.partial(per_device, mesh.shape["users"]),
        mesh=mesh,
        in_specs=in_specs,
        out_specs=P(spread, None),
        check_vma=False,
    )
```

```python
import functools
import math

import jax
import jax.numpy as jnp
from jax import lax
from jax.experimental import pallas as pl
from jax.experimental.pallas import tpu as pltpu
from jax.sharding import PartitionSpec as P

HEADS = 4
LANES = 128
FAR = -(2.0**60)
LINK = jnp.bfloat16
F32 = jnp.float32
BF16 = jnp.bfloat16


def divisor(total, wanted):
    return math.gcd(total, wanted)


def each_peer(n, body):
    if n <= 32:
        for i in sorted(range(1, n), key=lambda i: abs(i - n // 2)):
            body(i)
    else:
        pl.loop(1, n)(body)


def kernel(
    n,
    cand_hbm,
    cuser_hbm,
    ev_hbm,
    euser_hbm,
    emask_hbm,
    wq_hbm,
    wk_hbm,
    wv_hbm,
    wg_hbm,
    wo_hbm,
    out_ref,
    cand,
    cuser,
    ev,
    euser,
    emask,
    wq,
    wkv,
    wg,
    wo,
    q_own,
    q_all,
    users,
    hot,
    keys,
    vals,
    gate,
    own,
    part,
    land,
    in_sem,
    ev_sem,
    q_send,
    q_recv,
    u_send,
    u_recv,
    e_send,
    e_recv,
    r_send,
    r_recv,
):
    rows, width = cand.shape
    half = width // 2
    dh = width // HEADS
    pair = HEADS // 2
    events = ev.shape[1]
    chunk = divisor(events, 512)
    ev_chunks = events // chunk
    half_scale = 0.5 / math.sqrt(dh)

    me = lax.axis_index("users")
    c = lax.rem(me, 2)
    other = 1 - c
    sib_id = me - c + other
    sibling = {"users": sib_id}
    columns = pl.ds(pl.multiple_of(c * half, half), half)

    def peer_of(i):
        return lax.rem(me + i, n)

    small = [
        (cand_hbm, cand),
        (cuser_hbm, cuser),
        (wq_hbm, wq),
        (euser_hbm, euser.at[0]),
        (emask_hbm, emask.at[0]),
        (wk_hbm.at[:, columns], wkv.at[:, pl.ds(0, half)]),
        (wv_hbm.at[:, columns], wkv.at[:, pl.ds(half, half)]),
        (wg_hbm, wg),
        (wo_hbm, wo),
    ]
    copies = [pltpu.make_async_copy(s, d, in_sem.at[i]) for i, (s, d) in enumerate(small)]
    ev_copies = [
        pltpu.make_async_copy(
            ev_hbm.at[pl.ds(j * chunk, chunk)], ev.at[0, pl.ds(j * chunk, chunk)], ev_sem.at[j]
        )
        for j in range(ev_chunks)
    ]

    barrier = pltpu.get_barrier_semaphore()

    each_peer(
        n, lambda i: pl.semaphore_signal(barrier, inc=1, device_id={"users": peer_of(i)})
    )

    for copy in copies[:5]:
        copy.start()
    for copy in ev_copies:
        copy.start()
    for copy in copies[5:]:
        copy.start()

    for copy in copies[:3]:
        copy.wait()
    queries = jnp.dot(cand[...], wq[...], preferred_element_type=F32).astype(BF16)
    for core in range(2):
        q_own[core] = queries[:, core * half : (core + 1) * half]
    q_all[me] = q_own[c]
    users[me] = jnp.zeros((1, LANES), jnp.int32)
    users[me, :, pl.ds(0, rows)] = cuser[...]

    pl.semaphore_wait(barrier, n - 1)

    def q_copy(i):
        peer = peer_of(i)
        return pltpu.make_async_remote_copy(
            src_ref=q_own.at[lax.rem(peer, 2)],
            dst_ref=q_all.at[me],
            send_sem=q_send.at[0],
            recv_sem=q_recv.at[0],
            device_id={"users": peer},
        )

    def u_copy(i):
        peer = peer_of(i)
        return pltpu.make_async_remote_copy(
            src_ref=users.at[me],
            dst_ref=users.at[me],
            send_sem=u_send.at[0],
            recv_sem=u_recv.at[0],
            device_id={"users": peer},
        )

    def all_of(ref, send_sem, recv_sem):
        block = ref.at[pl.ds(0, n - 1)]
        return pltpu.make_async_remote_copy(
            src_ref=block,
            dst_ref=block,
            send_sem=send_sem,
            recv_sem=recv_sem,
            device_id=sibling,
        )

    all_q = all_of(q_all, q_send.at[0], q_recv.at[0])
    all_u = all_of(users, u_send.at[0], u_recv.at[0])

    def event_copy(j):
        at = pl.ds(j * chunk, chunk)
        return pltpu.make_async_remote_copy(
            src_ref=ev.at[0, at],
            dst_ref=ev.at[1, at],
            send_sem=e_send.at[j],
            recv_sem=e_recv.at[j],
            device_id=sibling,
        )

    def tag_copy(ref, j):
        return pltpu.make_async_remote_copy(
            src_ref=ref.at[0],
            dst_ref=ref.at[1],
            send_sem=e_send.at[j],
            recv_sem=e_recv.at[j],
            device_id=sibling,
        )

    handed = [event_copy(j) for j in range(ev_chunks)]
    tags = [tag_copy(euser, ev_chunks), tag_copy(emask, ev_chunks + 1)]
    each_peer(n, lambda i: q_copy(i).start())
    for local, copy in zip(ev_copies, handed):
        local.wait()
        copy.start()
    copies[3].wait()
    copies[4].wait()
    for copy in tags:
        copy.start()
    each_peer(n, lambda i: u_copy(i).start())

    def keys_and_values(e, chunks):
        for j in chunks:
            at = pl.ds(j * chunk, chunk)
            if e:
                handed[j].wait_recv()
            both = jnp.dot(ev[e, at, :], wkv[...], preferred_element_type=F32).astype(BF16)
            for h in range(pair):
                keys[h, e, at, pl.ds(0, dh)] = both[:, h * dh : (h + 1) * dh]
            vals[e, at, :] = both[:, half:]

    def mask_columns(e):
        for j in range(ev_chunks):
            at = pl.ds(j * chunk, chunk)
            eff = jnp.where(emask[e, :, at] == 1, euser[e, :, at], -1)
            ids = lax.broadcasted_iota(jnp.int32, (LANES, chunk), 0)
            miss = jnp.where(ids == eff, 0.0, FAR).T.astype(BF16)
            for h in range(pair):
                keys[h, e, at, pl.ds(dh, LANES)] = miss

    copies[5].wait()
    copies[6].wait()
    mask_columns(0)
    early = ev_chunks // 2
    keys_and_values(0, range(ev_chunks))

    copies[7].wait()
    pre = 0.5 * jnp.dot(cand[...], wg[...], preferred_element_type=F32)
    gate[...] = pre + pre * jnp.tanh(pre)
    copies[8].wait()

    for copy in tags:
        copy.wait_recv()
    mask_columns(1)
    keys_and_values(1, range(early))

    total = n * rows
    block = divisor(total, 256)
    slots = block // rows

    all_u.wait_recv()

    def one_hot(b):
        at_slots = pl.ds(b * slots, slots)
        shape = (slots, rows, LANES)
        own_lane = lax.broadcasted_iota(jnp.int32, shape, 1) == lax.broadcasted_iota(
            jnp.int32, shape, 2
        )
        spread = jnp.where(own_lane, jnp.broadcast_to(users[at_slots], shape).astype(F32), 0.0)
        user_col = jnp.sum(spread, axis=2, keepdims=True)
        lane_ids = lax.broadcasted_iota(jnp.int32, shape, 2).astype(F32)
        hot[at_slots] = jnp.where(lane_ids == user_col, 1.0, 0.0).astype(BF16)

    if total == block:
        one_hot(0)
    else:
        pl.loop(0, total // block)(one_hot)

    all_q.wait_recv()

    def attention(g, e, b):
        at_slots = pl.ds(b * slots, slots)
        q = q_all[at_slots].reshape(block, half)[:, g * dh : (g + 1) * dh]
        q = jnp.concatenate([q, hot[at_slots].reshape(block, LANES)], axis=1)
        acc = None
        for j in range(ev_chunks):
            at = pl.ds(j * chunk, chunk)
            raw = lax.dot_general(
                q, keys[g, e, at, :], (((1,), (1,)), ((), ())), preferred_element_type=F32
            )
            s = raw * half_scale
            attn = (s + s * jnp.tanh(s)).astype(BF16)
            term = jnp.dot(attn, vals[e, at, pl.ds(g * dh, dh)], preferred_element_type=F32)
            acc = term if acc is None else acc + term
        acc = acc.reshape(slots, rows, dh)
        if e:
            part[g, at_slots] = (own[g, at_slots] + acc).astype(LINK)
        else:
            own[g, at_slots] = acc

    def attend(g, e):
        if total == block:
            attention(g, e, 0)
        else:
            pl.loop(0, total // block)(functools.partial(attention, g, e))

    def give(g, i):
        peer = peer_of(i)
        return pltpu.make_async_remote_copy(
            src_ref=part.at[g, peer],
            dst_ref=land.at[g, me],
            send_sem=r_send.at[g],
            recv_sem=r_recv.at[g],
            device_id={"users": peer},
        )

    given = [all_of(land.at[g], r_send.at[g], r_recv.at[g]) for g in range(pair)]

    for g in range(pair):
        attend(g, 0)
    keys_and_values(1, range(early, ev_chunks))
    for g in range(pair):
        attend(g, 1)
        each_peer(n, functools.partial(lambda g, i: give(g, i).start(), g))
        land[g, me] = part[g, me]

    all_q.wait_send()
    all_u.wait_send()
    for copy in handed + tags:
        copy.wait_send()

    sums = []
    for g in range(pair):
        given[g].wait_recv()
        landed = land[g].astype(F32).reshape(n // 2, 2, rows, dh)
        sums.append(jnp.sum(landed, axis=0))
    summed = jnp.concatenate([sums[g][core] for core in range(2) for g in range(pair)], axis=1)
    mean = jnp.mean(summed, axis=1, keepdims=True)
    centred = summed - mean
    var = jnp.mean(centred * centred, axis=1, keepdims=True)
    normed = centred / jnp.sqrt(var + 1e-5)
    gated = (normed * gate[...]).astype(BF16)
    out_ref[...] = jnp.dot(gated, wo[...], preferred_element_type=F32)

    for copy in given:
        copy.wait_send()


def per_device(
    n,
    candidates,
    candidate_user,
    events,
    event_user,
    event_mask,
    query_weight,
    key_weight,
    value_weight,
    gate_weight,
    output_weight,
):
    rows, width = candidates.shape
    count = events.shape[0]
    half = width // 2
    pair = HEADS // 2
    dh = width // HEADS
    chunks = count // divisor(count, 512)
    square = pltpu.VMEM((width, width), BF16)
    dma = pltpu.SemaphoreType.DMA
    delta = pl.pallas_call(
        functools.partial(kernel, n),
        out_shape=jax.ShapeDtypeStruct((rows, width), F32),
        in_specs=[pl.BlockSpec(memory_space=pl.ANY)] * 10,
        out_specs=pl.BlockSpec(memory_space=pltpu.VMEM),
        scratch_shapes=[
            pltpu.VMEM((rows, width), BF16),
            pltpu.VMEM((1, rows), jnp.int32),
            pltpu.VMEM((2, count, width), BF16),
            pltpu.VMEM((2, 1, count), jnp.int32),
            pltpu.VMEM((2, 1, count), jnp.int32),
            square,
            square,
            square,
            square,
            pltpu.VMEM((2, rows, half), BF16),
            pltpu.VMEM((n, rows, half), BF16),
            pltpu.VMEM((n, 1, LANES), jnp.int32),
            pltpu.VMEM((n, rows, LANES), BF16),
            pltpu.VMEM((pair, 2, count, dh + LANES), BF16),
            pltpu.VMEM((2, count, half), BF16),
            pltpu.VMEM((rows, width), F32),
            pltpu.VMEM((pair, n, rows, dh), F32),
            pltpu.VMEM((pair, n, rows, dh), LINK),
            pltpu.VMEM((pair, n, rows, dh), LINK),
            dma((9,)),
            dma((chunks,)),
            dma((1,)),
            dma((1,)),
            dma((1,)),
            dma((1,)),
            dma((chunks + 2,)),
            dma((chunks + 2,)),
            dma((pair,)),
            dma((pair,)),
        ],
        compiler_params=pltpu.CompilerParams(
            collective_id=0, has_side_effects=True, vmem_limit_bytes=56 * 2**20
        ),
    )(
        candidates,
        candidate_user.reshape(1, rows),
        events,
        event_user.reshape(1, count),
        event_mask.reshape(1, count),
        query_weight,
        key_weight,
        value_weight,
        gate_weight,
        output_weight,
    )
    return (candidates.astype(F32) + delta).astype(BF16)


def solution(mesh):
    spread = ("parts", "users")
    in_specs = (P(spread, None), P(spread), P(spread, None), P(spread), P(spread)) + (P(),) * 5
    return jax.shard_map(
        functools.partial(per_device, mesh.shape["users"]),
        mesh=mesh,
        in_specs=in_specs,
        out_specs=P(spread, None),
        check_vma=False,
    )
```

```python
import functools
import math

import jax
import jax.numpy as jnp
from jax import lax
from jax.experimental import pallas as pl
from jax.experimental.pallas import tpu as pltpu
from jax.sharding import PartitionSpec as P

HEADS = 4
LANES = 128
FAR = -(2.0**60)
LINK = jnp.bfloat16
F32 = jnp.float32
BF16 = jnp.bfloat16


def divisor(total, wanted):
    return math.gcd(total, wanted)


def each_peer(n, body):
    if n <= 32:
        for i in sorted(range(1, n), key=lambda i: abs(i - n // 2)):
            body(i)
    else:
        pl.loop(1, n)(body)


def kernel(
    n,
    cand_hbm,
    cuser_hbm,
    ev_hbm,
    euser_hbm,
    emask_hbm,
    wq_hbm,
    wk_hbm,
    wv_hbm,
    wg_hbm,
    wo_hbm,
    out_ref,
    cand,
    cuser,
    ev,
    euser,
    emask,
    wq,
    wkv,
    wg,
    wo,
    q_own,
    q_all,
    users,
    hot,
    keys,
    vals,
    gate,
    part,
    land,
    in_sem,
    ev_sem,
    q_send,
    q_recv,
    u_send,
    u_recv,
    e_send,
    e_recv,
    r_send,
    r_recv,
):
    rows, width = cand.shape
    half = width // 2
    dh = width // HEADS
    pair = HEADS // 2
    events = ev.shape[1]
    chunk = divisor(events, 512)
    ev_chunks = events // chunk
    half_scale = 0.5 / math.sqrt(dh)

    me = lax.axis_index("users")
    c = lax.rem(me, 2)
    other = 1 - c
    sib_id = me - c + other
    sibling = {"users": sib_id}
    columns = pl.ds(pl.multiple_of(c * half, half), half)

    def peer_of(i):
        return lax.rem(me + i, n)

    small = [
        (cand_hbm, cand),
        (cuser_hbm, cuser),
        (wq_hbm, wq),
        (euser_hbm, euser.at[0]),
        (emask_hbm, emask.at[0]),
        (wk_hbm.at[:, columns], wkv.at[:, pl.ds(0, half)]),
        (wv_hbm.at[:, columns], wkv.at[:, pl.ds(half, half)]),
        (wg_hbm, wg),
        (wo_hbm, wo),
    ]
    copies = [pltpu.make_async_copy(s, d, in_sem.at[i]) for i, (s, d) in enumerate(small)]
    ev_copies = [
        pltpu.make_async_copy(
            ev_hbm.at[pl.ds(j * chunk, chunk)], ev.at[0, pl.ds(j * chunk, chunk)], ev_sem.at[j]
        )
        for j in range(ev_chunks)
    ]

    barrier = pltpu.get_barrier_semaphore()

    each_peer(
        n, lambda i: pl.semaphore_signal(barrier, inc=1, device_id={"users": peer_of(i)})
    )

    for copy in copies[:5]:
        copy.start()
    for copy in ev_copies:
        copy.start()
    for copy in copies[5:]:
        copy.start()

    for copy in copies[:3]:
        copy.wait()
    queries = jnp.dot(cand[...], wq[...], preferred_element_type=F32).astype(BF16)
    for core in range(2):
        q_own[core] = queries[:, core * half : (core + 1) * half]
    q_all[me] = q_own[c]
    users[me] = jnp.zeros((1, LANES), jnp.int32)
    users[me, :, pl.ds(0, rows)] = cuser[...]

    pl.semaphore_wait(barrier, n - 1)

    def q_copy(i):
        peer = peer_of(i)
        return pltpu.make_async_remote_copy(
            src_ref=q_own.at[lax.rem(peer, 2)],
            dst_ref=q_all.at[me],
            send_sem=q_send.at[0],
            recv_sem=q_recv.at[0],
            device_id={"users": peer},
        )

    def u_copy(i):
        peer = peer_of(i)
        return pltpu.make_async_remote_copy(
            src_ref=users.at[me],
            dst_ref=users.at[me],
            send_sem=u_send.at[0],
            recv_sem=u_recv.at[0],
            device_id={"users": peer},
        )

    def all_of(ref, send_sem, recv_sem):
        block = ref.at[pl.ds(0, n - 1)]
        return pltpu.make_async_remote_copy(
            src_ref=block,
            dst_ref=block,
            send_sem=send_sem,
            recv_sem=recv_sem,
            device_id=sibling,
        )

    all_q = all_of(q_all, q_send.at[0], q_recv.at[0])
    all_u = all_of(users, u_send.at[0], u_recv.at[0])

    def event_copy(j):
        at = pl.ds(j * chunk, chunk)
        return pltpu.make_async_remote_copy(
            src_ref=ev.at[0, at],
            dst_ref=ev.at[1, at],
            send_sem=e_send.at[j],
            recv_sem=e_recv.at[j],
            device_id=sibling,
        )

    def tag_copy(ref, j):
        return pltpu.make_async_remote_copy(
            src_ref=ref.at[0],
            dst_ref=ref.at[1],
            send_sem=e_send.at[j],
            recv_sem=e_recv.at[j],
            device_id=sibling,
        )

    handed = [event_copy(j) for j in range(ev_chunks)]
    tags = [tag_copy(euser, ev_chunks), tag_copy(emask, ev_chunks + 1)]
    each_peer(n, lambda i: q_copy(i).start())
    each_peer(n, lambda i: u_copy(i).start())
    for local, copy in zip(ev_copies, handed):
        local.wait()
        copy.start()
    copies[3].wait()
    copies[4].wait()
    for copy in tags:
        copy.start()

    def keys_and_values(e):
        for j in range(ev_chunks):
            at = pl.ds(j * chunk, chunk)
            if e:
                handed[j].wait_recv()
            both = jnp.dot(ev[e, at, :], wkv[...], preferred_element_type=F32).astype(BF16)
            for h in range(pair):
                keys[h, e, at, pl.ds(0, dh)] = both[:, h * dh : (h + 1) * dh]
            vals[e, at, :] = both[:, half:]

    def mask_columns(e):
        for j in range(ev_chunks):
            at = pl.ds(j * chunk, chunk)
            eff = jnp.where(emask[e, :, at] == 1, euser[e, :, at], -1)
            ids = lax.broadcasted_iota(jnp.int32, (LANES, chunk), 0)
            miss = jnp.where(ids == eff, 0.0, FAR).T.astype(BF16)
            for h in range(pair):
                keys[h, e, at, pl.ds(dh, LANES)] = miss

    copies[5].wait()
    copies[6].wait()
    mask_columns(0)
    keys_and_values(0)

    copies[7].wait()
    pre = 0.5 * jnp.dot(cand[...], wg[...], preferred_element_type=F32)
    gate[...] = pre + pre * jnp.tanh(pre)
    copies[8].wait()

    for copy in tags:
        copy.wait_recv()
    mask_columns(1)
    keys_and_values(1)

    total = n * rows
    block = divisor(total, 256)
    slots = block // rows

    all_u.wait_recv()

    def one_hot(b):
        at_slots = pl.ds(b * slots, slots)
        shape = (slots, rows, LANES)
        own_lane = lax.broadcasted_iota(jnp.int32, shape, 1) == lax.broadcasted_iota(
            jnp.int32, shape, 2
        )
        spread = jnp.where(own_lane, jnp.broadcast_to(users[at_slots], shape).astype(F32), 0.0)
        user_col = jnp.sum(spread, axis=2, keepdims=True)
        lane_ids = lax.broadcasted_iota(jnp.int32, shape, 2).astype(F32)
        hot[at_slots] = jnp.where(lane_ids == user_col, 1.0, 0.0).astype(BF16)

    if total == block:
        one_hot(0)
    else:
        pl.loop(0, total // block)(one_hot)

    all_q.wait_recv()

    def attention(g, b):
        at_slots = pl.ds(b * slots, slots)
        q = q_all[at_slots].reshape(block, half)[:, g * dh : (g + 1) * dh]
        q = jnp.concatenate([q, hot[at_slots].reshape(block, LANES)], axis=1)
        acc = None
        for e in range(2):
            for j in range(ev_chunks):
                at = pl.ds(j * chunk, chunk)
                raw = lax.dot_general(
                    q, keys[g, e, at, :], (((1,), (1,)), ((), ())), preferred_element_type=F32
                )
                s = raw * half_scale
                attn = (s + s * jnp.tanh(s)).astype(BF16)
                term = jnp.dot(
                    attn, vals[e, at, pl.ds(g * dh, dh)], preferred_element_type=F32
                )
                acc = term if acc is None else acc + term
        part[g, at_slots] = acc.reshape(slots, rows, dh).astype(LINK)

    def give(g, i):
        peer = peer_of(i)
        return pltpu.make_async_remote_copy(
            src_ref=part.at[g, peer],
            dst_ref=land.at[g, me],
            send_sem=r_send.at[g],
            recv_sem=r_recv.at[g],
            device_id={"users": peer},
        )

    given = [all_of(land.at[g], r_send.at[g], r_recv.at[g]) for g in range(pair)]

    for g in range(pair):
        if total == block:
            attention(g, 0)
        else:
            pl.loop(0, total // block)(functools.partial(attention, g))

        each_peer(n, functools.partial(lambda g, i: give(g, i).start(), g))
        land[g, me] = part[g, me]

    all_q.wait_send()
    all_u.wait_send()
    for copy in handed + tags:
        copy.wait_send()

    sums = []
    for g in range(pair):
        given[g].wait_recv()
        landed = land[g].astype(F32).reshape(n // 2, 2, rows, dh)
        sums.append(jnp.sum(landed, axis=0))
    summed = jnp.concatenate([sums[g][core] for core in range(2) for g in range(pair)], axis=1)
    mean = jnp.mean(summed, axis=1, keepdims=True)
    centred = summed - mean
    var = jnp.mean(centred * centred, axis=1, keepdims=True)
    normed = centred / jnp.sqrt(var + 1e-5)
    gated = (normed * gate[...]).astype(BF16)
    out_ref[...] = jnp.dot(gated, wo[...], preferred_element_type=F32)

    for copy in given:
        copy.wait_send()


def per_device(
    n,
    candidates,
    candidate_user,
    events,
    event_user,
    event_mask,
    query_weight,
    key_weight,
    value_weight,
    gate_weight,
    output_weight,
):
    rows, width = candidates.shape
    count = events.shape[0]
    half = width // 2
    pair = HEADS // 2
    dh = width // HEADS
    chunks = count // divisor(count, 512)
    square = pltpu.VMEM((width, width), BF16)
    dma = pltpu.SemaphoreType.DMA
    delta = pl.pallas_call(
        functools.partial(kernel, n),
        out_shape=jax.ShapeDtypeStruct((rows, width), F32),
        in_specs=[pl.BlockSpec(memory_space=pl.ANY)] * 10,
        out_specs=pl.BlockSpec(memory_space=pltpu.VMEM),
        scratch_shapes=[
            pltpu.VMEM((rows, width), BF16),
            pltpu.VMEM((1, rows), jnp.int32),
            pltpu.VMEM((2, count, width), BF16),
            pltpu.VMEM((2, 1, count), jnp.int32),
            pltpu.VMEM((2, 1, count), jnp.int32),
            square,
            square,
            square,
            square,
            pltpu.VMEM((2, rows, half), BF16),
            pltpu.VMEM((n, rows, half), BF16),
            pltpu.VMEM((n, 1, LANES), jnp.int32),
            pltpu.VMEM((n, rows, LANES), BF16),
            pltpu.VMEM((pair, 2, count, dh + LANES), BF16),
            pltpu.VMEM((2, count, half), BF16),
            pltpu.VMEM((rows, width), F32),
            pltpu.VMEM((pair, n, rows, dh), LINK),
            pltpu.VMEM((pair, n, rows, dh), LINK),
            dma((9,)),
            dma((chunks,)),
            dma((1,)),
            dma((1,)),
            dma((1,)),
            dma((1,)),
            dma((chunks + 2,)),
            dma((chunks + 2,)),
            dma((pair,)),
            dma((pair,)),
        ],
        compiler_params=pltpu.CompilerParams(
            collective_id=0, has_side_effects=True, vmem_limit_bytes=56 * 2**20
        ),
    )(
        candidates,
        candidate_user.reshape(1, rows),
        events,
        event_user.reshape(1, count),
        event_mask.reshape(1, count),
        query_weight,
        key_weight,
        value_weight,
        gate_weight,
        output_weight,
    )
    return (candidates.astype(F32) + delta).astype(BF16)


def solution(mesh):
    spread = ("parts", "users")
    in_specs = (P(spread, None), P(spread), P(spread, None), P(spread), P(spread)) + (P(),) * 5
    return jax.shard_map(
        functools.partial(per_device, mesh.shape["users"]),
        mesh=mesh,
        in_specs=in_specs,
        out_specs=P(spread, None),
        check_vma=False,
    )
```
